32 devices in a mesh: lat: 8 (over z, x), lev: 4 (over y, core).
Axes of the slice: x: 2, y: 2, z: 4, core: 2. Of those that a mesh axis runs over, the one named last changes fastest.
Arguments:
- particle_mass_fraction: float32 [20, 64, 8, 360], P(None, 'lat', 'lev'), may hold values from 0.1 to 2
- meridional_cfl_factor: float32 [64, 8, 360], P('lat', 'lev'), may hold values from -0.45 to 0.45
- thermal_state_kelvins: float32 [64, 8, 360], P('lat', 'lev'), may hold values from 200 to 300
- logarithmic_barometric_span: float32 [8], P('lev'), may hold values from 0.06 to 0.2
- gravitational_fall_kilometres: float32 [20], replicated, may hold values from 0.02 to 20
- zonal_cfl_factor: float32 [64, 8, 360], P('lat', None, 'lev'), may hold values from -0.45 to 0.45
- collision_rate_matrix: float32 [20, 20], replicated, may hold values from 0.02 to 0.2
Outputs:
- dust_out: float32 [20, 64, 8, 360], P(None, 'lat', None, 'lev')
- height: float32 [64, 8, 360], P('lat', 'lev')
The draws below stay inside these ranges and needn't reach their ends.
All inputs are finite; a program needn't handle non-finite values.
Results may differ from the reference program's by a relative error of at most 0.000067.
Values sent between devices are 32-bit elements; how exact they have to be, the bound alone decides.
A program may use at most 128 MiB of HBM per device.

```python
import math
import jax
import jax.numpy as jnp
from jax import lax

BINS = 20
MERIDIAN_POINTS = 64
VERTICAL_TIERS = 8
ZONAL_POINTS = 360


def level_of(own_key, extent, cuts, low, largest):
    loudness, own = 1.0, jax.random.fold_in(own_key, 6)
    for dim, shards_of in cuts:
        heights = jnp.exp(jax.random.uniform(jax.random.fold_in(own, dim), (shards_of,), jnp.float32, low / len(cuts), largest / len(cuts)))
        loudness = loudness * jnp.repeat(heights, extent[dim] // shards_of).reshape([-1 if axis == dim else 1 for axis in range(len(extent))])
    return loudness


def setup_inputs(seed: int = 0) -> dict:
    keys = jax.random.split(jax.random.key(seed), 8)
    particle_mass_fraction = jnp.clip(jnp.exp(math.log(2.0) - 2.9957323 * jax.random.uniform(keys[0], (BINS, MERIDIAN_POINTS, VERTICAL_TIERS, ZONAL_POINTS), jnp.float32) ** level_of(keys[0], (BINS, MERIDIAN_POINTS, VERTICAL_TIERS, ZONAL_POINTS), ((1, 8), (2, 4)), -0.2, 0.2)), 0.1, 2.0)
    meridional_cfl_factor = jnp.clip(jax.random.uniform(keys[1], (MERIDIAN_POINTS, VERTICAL_TIERS, ZONAL_POINTS), jnp.float32, -0.45, 0.45) * level_of(keys[1], (MERIDIAN_POINTS, VERTICAL_TIERS, ZONAL_POINTS), ((0, 8), (1, 4)), -0.4, 0.0), -0.45, 0.45)
    thermal_state_kelvins = jnp.clip(200.0 + 100.0 * jax.random.uniform(keys[2], (MERIDIAN_POINTS, VERTICAL_TIERS, ZONAL_POINTS), jnp.float32) ** level_of(keys[2], (MERIDIAN_POINTS, VERTICAL_TIERS, ZONAL_POINTS), ((0, 8), (1, 4)), -0.2, 0.2), 200.0, 300.0)
    logarithmic_barometric_span = jnp.clip(jnp.exp(math.log(0.2) - 1.2039728 * jax.random.uniform(keys[3], (VERTICAL_TIERS,), jnp.float32) ** level_of(keys[3], (VERTICAL_TIERS,), ((0, 4),), -0.2, 0.2)), 0.06, 0.2)
    gravitational_fall_kilometres = jnp.clip(jnp.exp(jax.random.uniform(keys[4], (BINS,), jnp.float32, math.log(0.02), math.log(20.0))), 0.02, 20.0)
    zonal_cfl_factor = jnp.clip(jax.random.uniform(keys[5], (MERIDIAN_POINTS, VERTICAL_TIERS, ZONAL_POINTS), jnp.float32, -0.45, 0.45) * level_of(keys[5], (MERIDIAN_POINTS, VERTICAL_TIERS, ZONAL_POINTS), ((0, 8), (2, 4)), -0.4, 0.0), -0.45, 0.45)
    collision_rate_matrix = jnp.clip(jnp.exp(jax.random.uniform(keys[6], (BINS, BINS), jnp.float32, math.log(0.02), math.log(0.2))), 0.02, 0.2)
    return {"particle_mass_fraction": particle_mass_fraction, "meridional_cfl_factor": meridional_cfl_factor, "thermal_state_kelvins": thermal_state_kelvins, "logarithmic_barometric_span": logarithmic_barometric_span, "gravitational_fall_kilometres": gravitational_fall_kilometres, "zonal_cfl_factor": zonal_cfl_factor, "collision_rate_matrix": collision_rate_matrix}


specific_air_factor = 0.0293
scale_height = 7.0


def settle_sweep(mixing, settle_rate, inflow):
    def stepper(flux_in, inputs):
        level_mix, level_rate = inputs
        summed = level_mix + flux_in
        return level_rate / (1.0 + level_rate) * summed, summed / (1.0 + level_rate)

    _, swept = lax.scan(stepper, inflow, (jnp.moveaxis(mixing, 2, 0), jnp.moveaxis(settle_rate, 2, 0)))
    return jnp.moveaxis(swept, 0, 2)


def reference(particle_mass_fraction, meridional_cfl_factor, thermal_state_kelvins, logarithmic_barometric_span, gravitational_fall_kilometres, zonal_cfl_factor, collision_rate_matrix):
    rows_below = jnp.pad(particle_mass_fraction, ((0, 0), (1, 0), (0, 0), (0, 0)))[:, :-1]
    south_flux = jnp.maximum(meridional_cfl_factor, 0.0) * rows_below + jnp.minimum(meridional_cfl_factor, 0.0) * particle_mass_fraction
    north_flux = jnp.pad(south_flux, ((0, 0), (0, 1), (0, 0), (0, 0)))[:, 1:]
    advected = particle_mass_fraction + south_flux - north_flux
    vertical_span_height = specific_air_factor * thermal_state_kelvins * logarithmic_barometric_span[None, :, None]
    height = jnp.cumsum(vertical_span_height[:, ::-1], axis=1)[:, ::-1] - 0.5 * vertical_span_height
    density = jnp.exp(-height / scale_height)
    settle_rate = gravitational_fall_kilometres[:, None, None, None] / vertical_span_height[None]
    inflow = jnp.zeros((particle_mass_fraction.shape[0], particle_mass_fraction.shape[1], particle_mass_fraction.shape[3]), jnp.float32)
    settled = settle_sweep(advected, settle_rate, inflow)
    west_mix = jnp.roll(settled, 1, axis=3)
    west_flux = jnp.maximum(zonal_cfl_factor, 0.0) * west_mix + jnp.minimum(zonal_cfl_factor, 0.0) * settled
    east_flux = jnp.roll(west_flux, -1, axis=3)
    moved = settled + west_flux - east_flux
    merging = jnp.tril(collision_rate_matrix, -1) - jnp.triu(collision_rate_matrix, 1)
    coag_rate = jnp.einsum("bc,clkx->blkx", merging, moved, precision=lax.Precision.HIGHEST)
    return moved + density * moved * coag_rate, height
```

```python
import functools

import jax
import jax.numpy as jnp
from jax import lax
from jax.experimental import pallas as pl
from jax.experimental.pallas import tpu as pltpu
from jax.sharding import PartitionSpec as P

specific_air_factor = 0.0293
scale_height = 7.0
LANES = 128
MESH = pl.DeviceIdType.MESH
HIGHEST = lax.Precision.HIGHEST


def widen(x):
    short = -x.shape[-1] % LANES
    if short:
        x = jnp.concatenate([x, jnp.zeros((*x.shape[:-1], short), x.dtype)], -1)
    return x


def lon_block(tile, total, width, block):
    axis = 2
    count = -(-total // LANES)
    last = total % LANES
    start = block * width - 1
    c, off = start // LANES, start % LANES

    def piece(i):
        if i < 0:
            return pltpu.roll(tile(count - 1), (LANES - last) % LANES, axis)
        if i == count:
            return tile(0)
        x = tile(i)
        if i == count - 1 and last and total < start + width + 2:
            lane = lax.broadcasted_iota(jnp.int32, x.shape, axis)
            x = jnp.where(lane < last, x, pltpu.roll(tile(0), last, axis))
        return x

    x = piece(c)
    if off + width + 2 > LANES:
        lane = lax.broadcasted_iota(jnp.int32, x.shape, axis)
        x = jnp.where(lane >= off, x, piece(c + 1))
    return pltpu.roll(x, (2 * LANES - off - 1) % LANES, axis)


def kernel(
    n_lat, n_lev,
    q_ref, mc_ref, temp_ref, span_ref, fall_ref, zc_ref, rate_ref,
    out_ref, height_ref,
    main_s, main_r, thick_s, thick_r, north_s, north_r, south_s, south_r,
    tot_s, tot_r, zc_s, zc_r, fall_v, kron, dens,
    main_ss, main_rs, thick_ss, thick_rs, north_ss, north_rs, south_ss, south_rs,
    tot_ss, tot_rs, zc_sem, own_sem,
):
    i, j = lax.axis_index("lat"), lax.axis_index("lev")
    bins, rows, levels, total = q_ref.shape
    width = total // n_lev
    left, right = lax.rem(j + n_lev - 1, n_lev), lax.rem(j + 1, n_lev)
    has_south, has_north = i > 0, i < n_lat - 1

    barrier = pltpu.get_barrier_semaphore()
    for d in range(1, n_lev):
        pl.semaphore_signal(barrier, inc=1, device_id=(i, lax.rem(j + d, n_lev)), device_id_type=MESH)

    @pl.when(has_south)
    def _():
        for m in range(n_lev):
            pl.semaphore_signal(barrier, inc=1, device_id=(i - 1, m), device_id_type=MESH)

    @pl.when(has_north)
    def _():
        for m in range(n_lev):
            pl.semaphore_signal(barrier, inc=1, device_id=(i + 1, m), device_id_type=MESH)

    thick = [specific_air_factor * temp_ref[:, k, :] * span_ref[k] for k in range(levels)]
    tot = thick[0]
    for k in range(1, levels):
        tot = tot + thick[k]
    tot_s[...] = widen(tot)
    for m in range(n_lev):
        for k in range(levels):
            wide = widen(thick[k])[None]
            tile = lambda c: wide[:, :, c * LANES : (c + 1) * LANES]
            thick_s[m, k] = lon_block(tile, total, width, m)[0]
    zc_s[...] = widen(zc_ref[...])

    peers = n_lev - 1 + n_lev * (jnp.minimum(i, 1) + jnp.minimum(n_lat - 1 - i, 1))
    pl.semaphore_wait(barrier, peers)

    def thick_copy(m):
        return pltpu.make_async_remote_copy(
            thick_s.at[m], thick_r.at[j], thick_ss.at[m], thick_rs.at[j], (i, m), MESH)

    def main_copy(m):
        return pltpu.make_async_remote_copy(
            main_s.at[m], main_r.at[j], main_ss.at[m], main_rs.at[j], (i, m), MESH)

    def tot_copy(m):
        return pltpu.make_async_remote_copy(
            tot_s, tot_r.at[j], tot_ss.at[m], tot_rs.at[j], (i, m), MESH)

    def north_copy(m):
        return pltpu.make_async_remote_copy(
            north_s.at[m], north_r.at[j], north_ss.at[m], north_rs.at[j], (i + 1, m), MESH)

    def south_copy(m):
        return pltpu.make_async_remote_copy(
            south_s.at[m], south_r.at[j], south_ss.at[m], south_rs.at[j], (i - 1, m), MESH)

    zc_copy = pltpu.make_async_remote_copy(
        zc_s, zc_r, zc_sem.at[0], zc_sem.at[1], (i, left), MESH)

    for m in range(n_lev):
        @pl.when(j != m)
        def _():
            thick_copy(m).start()
    zc_copy.start()

    last = total - (total // LANES) * LANES

    def tile_of(ref, k):
        def tile(c):
            stop = min((c + 1) * LANES, total)
            return widen(ref[:, :, k, c * LANES : stop])
        return tile

    def mc_tile(k):
        def tile(c):
            stop = min((c + 1) * LANES, total)
            return widen(mc_ref[:, k, c * LANES : stop])[None]
        return tile

    for m in range(n_lev):
        for k in range(levels):
            main_s[m, k, pl.ds(0, bins)] = lon_block(tile_of(q_ref, k), total, width, m)
            main_s[m, k, pl.ds(bins, 1)] = lon_block(mc_tile(k), total, width, m)

        @pl.when(j != m)
        def _():
            main_copy(m).start()

        for k in range(levels):
            south_s[m, k, pl.ds(0, bins + 1)] = main_s[m, k, :, 0, :]
            north_s[m, k, pl.ds(0, bins + 1)] = main_s[m, k, :, rows - 1, :]
        pad = south_s.shape[2] - bins - 1
        if pad:
            zero = jnp.zeros((levels, pad, LANES), jnp.float32)
            south_s[m, :, pl.ds(bins + 1, pad)] = zero
            north_s[m, :, pl.ds(bins + 1, pad)] = zero

        @pl.when(has_south)
        def _():
            south_copy(m).start()

        @pl.when(has_north)
        def _():
            north_copy(m).start()

    for m in range(n_lev):
        @pl.when(j != m)
        def _():
            tot_copy(m).start()

    own = [pltpu.make_async_copy(main_s.at[j], main_r.at[j], own_sem.at[0]),
           pltpu.make_async_copy(thick_s.at[j], thick_r.at[j], own_sem.at[1])]
    for copy in own:
        copy.start()

    @pl.when(jnp.logical_not(has_south))
    def _():
        north_r[...] = jnp.zeros_like(north_r)

    @pl.when(jnp.logical_not(has_north))
    def _():
        south_r[...] = jnp.zeros_like(south_r)

    for b in range(bins):
        fall_v[b] = jnp.full((rows, LANES), fall_ref[b], jnp.float32)
    rate = rate_ref[...]
    r0 = lax.broadcasted_iota(jnp.int32, rate.shape, 0)
    r1 = lax.broadcasted_iota(jnp.int32, rate.shape, 1)
    merging = jnp.where(r1 < r0, rate, jnp.where(r1 > r0, -rate, 0.0))
    cells = bins * rows
    e0 = lax.broadcasted_iota(jnp.int32, (cells, bins), 0)
    e1 = lax.broadcasted_iota(jnp.int32, (cells, bins), 1)
    spread = jnp.where((e0 >= e1 * rows) & (e0 < (e1 + 1) * rows), 1.0, 0.0)
    half = jnp.dot(spread, merging, precision=HIGHEST, preferred_element_type=jnp.float32)
    full = lax.dot_general(half, spread, (((1,), (1,)), ((), ())), precision=HIGHEST,
                           preferred_element_type=jnp.float32)
    k0 = lax.broadcasted_iota(jnp.int32, full.shape, 0)
    k1 = lax.broadcasted_iota(jnp.int32, full.shape, 1)
    kron[...] = jnp.where(lax.rem(k0, rows) == lax.rem(k1, rows), full, 0.0)

    own[1].wait()
    for m in range(n_lev):
        @pl.when(j != m)
        def _():
            pltpu.make_async_remote_copy(
                thick_s.at[m], thick_r.at[m], thick_ss.at[m], thick_rs.at[m], (i, m), MESH).wait_recv()
    below = jnp.zeros((rows, LANES), jnp.float32)
    for k in reversed(range(n_lev * levels)):
        t = thick_r[k // levels, k % levels]
        dens[k] = jnp.exp((below + 0.5 * t) * (-1.0 / scale_height))
        below = below + t

    own[0].wait()
    zc_copy.wait_recv()

    flow = jnp.zeros((bins, rows, LANES), jnp.float32)
    sub = lax.broadcasted_iota(jnp.int32, (1, rows, LANES), 1)
    lane = lax.broadcasted_iota(jnp.int32, (1, rows, LANES), 2)
    for m in range(n_lev):
        @pl.when(j != m)
        def _():
            pltpu.make_async_remote_copy(
                main_s.at[m], main_r.at[m], main_ss.at[m], main_rs.at[m], (i, m), MESH).wait_recv()

        @pl.when(has_south)
        def _():
            pltpu.make_async_remote_copy(
                north_s.at[m], north_r.at[m], north_ss.at[m], north_rs.at[m], (i - 1, m), MESH).wait_recv()

        @pl.when(has_north)
        def _():
            pltpu.make_async_remote_copy(
                south_s.at[m], south_r.at[m], south_ss.at[m], south_rs.at[m], (i + 1, m), MESH).wait_recv()

        for kk in range(levels):
            k = m * levels + kk
            q = main_r[m, kk, pl.ds(0, bins)]
            mc = main_r[m, kk, pl.ds(bins, 1)]
            t = thick_r[m, pl.ds(kk, 1)]
            q_below = north_r[m, kk, pl.ds(0, bins)][:, None, :]
            q_above = south_r[m, kk, pl.ds(0, bins)][:, None, :]
            mc_above = south_r[m, kk, pl.ds(bins, 1)][:, None, :]
            q_s = jnp.where(sub == 0, q_below, pltpu.roll(q, 1, 1))
            q_n = jnp.where(sub == rows - 1, q_above, pltpu.roll(q, rows - 1, 1))
            mc_n = jnp.where(sub == rows - 1, mc_above, pltpu.roll(mc, rows - 1, 1))
            south = jnp.maximum(mc, 0.0) * q_s + jnp.minimum(mc, 0.0) * q
            north = jnp.maximum(mc_n, 0.0) * q + jnp.minimum(mc_n, 0.0) * q_n
            summed = (q + south - north) + flow
            f = fall_v[...]
            part = summed / (t + f)
            settled = t * part
            flow = f * part
            z = jnp.where(lane == width, pltpu.roll(zc_r[:, k, :][None], width, 2), zc_s[:, k, :][None])
            west = jnp.maximum(z, 0.0) * pltpu.roll(settled, 1, 2) + jnp.minimum(z, 0.0) * settled
            moved = settled + west - pltpu.roll(west, LANES - 1, 2)
            coag = jnp.dot(kron[...], moved.reshape(cells, LANES), precision=HIGHEST,
                           preferred_element_type=jnp.float32).reshape(moved.shape)
            result = moved + dens[pl.ds(k, 1)] * moved * coag
            out_ref[:, :, k, :] = result[:, :, :width]

    below = jnp.zeros((rows, total), jnp.float32)
    for m in range(n_lev):
        @pl.when(j != m)
        def _():
            pltpu.make_async_remote_copy(
                tot_s, tot_r.at[m], tot_ss.at[m], tot_rs.at[m], (i, m), MESH).wait_recv()

        @pl.when(j >= m)
        def _():
            tot_r[m] = jnp.zeros_like(tot_s)
        below = below + tot_r[m][:, :total]
    for k in reversed(range(levels)):
        t = specific_air_factor * temp_ref[:, k, :] * span_ref[k]
        height_ref[:, k, :] = below + 0.5 * t
        below = below + t

    zc_copy.wait_send()
    for m in range(n_lev):
        @pl.when(j != m)
        def _():
            thick_copy(m).wait_send()
            main_copy(m).wait_send()
            tot_copy(m).wait_send()

        @pl.when(has_south)
        def _():
            south_copy(m).wait_send()

        @pl.when(has_north)
        def _():
            north_copy(m).wait_send()


def solution(mesh):
    n_lat, n_lev = mesh.shape["lat"], mesh.shape["lev"]
    vmem = pl.BlockSpec(memory_space=pltpu.VMEM)
    smem = pl.BlockSpec(memory_space=pltpu.SMEM)

    def on_device(q, mc, temp, span, fall, zc, rate):
        bins, rows, levels, total = q.shape
        width = total // n_lev
        assert width + 2 <= LANES
        n_edge = -(-(bins + 1) // 8) * 8
        deep = n_lev * levels
        wide = -(-total // LANES) * LANES
        f32 = jnp.float32
        main = pltpu.VMEM((n_lev, levels, bins + 1, rows, LANES), f32)
        thick = pltpu.VMEM((n_lev, levels, rows, LANES), f32)
        edge = pltpu.VMEM((n_lev, levels, n_edge, LANES), f32)
        zonal = pltpu.VMEM((rows, deep, LANES), f32)
        sems = pltpu.SemaphoreType.DMA((n_lev,))
        pair = pltpu.SemaphoreType.DMA((2,))
        return pl.pallas_call(
            functools.partial(kernel, n_lat, n_lev),
            out_shape=(
                jax.ShapeDtypeStruct((bins, rows, deep, width), f32),
                jax.ShapeDtypeStruct((rows, levels, total), f32),
            ),
            in_specs=[vmem, vmem, vmem, smem, smem, vmem, vmem],
            out_specs=(vmem, vmem),
            scratch_shapes=[
                main, main, thick, thick, edge, edge, edge, edge,
                pltpu.VMEM((rows, wide), f32), pltpu.VMEM((n_lev, rows, wide), f32),
                zonal, zonal,
                pltpu.VMEM((bins, rows, LANES), f32),
                pltpu.VMEM((bins * rows, bins * rows), f32),
                pltpu.VMEM((deep, rows, LANES), f32),
            ] + [sems] * 10 + [pair] * 2,
            compiler_params=pltpu.CompilerParams(
                collective_id=0, has_side_effects=True, vmem_limit_bytes=48 * 1024 * 1024),
        )(q, mc, temp, span, fall, zc, rate)

    in_specs = (
        P(None, "lat", "lev", None),
        P("lat", "lev", None),
        P("lat", "lev", None),
        P("lev"),
        P(),
        P("lat", None, "lev"),
        P(),
    )
    out_specs = (P(None, "lat", None, "lev"), P("lat", "lev", None))
    return jax.shard_map(
        on_device, mesh=mesh, in_specs=in_specs, out_specs=out_specs, check_vma=False
    )
```

```python
import functools

import jax
import jax.numpy as jnp
from jax import lax
from jax.experimental import pallas as pl
from jax.experimental.pallas import tpu as pltpu
from jax.sharding import PartitionSpec as P

specific_air_factor = 0.0293
scale_height = 7.0
LANES = 128
MESH = pl.DeviceIdType.MESH
HIGHEST = lax.Precision.HIGHEST


def widen(x):
    short = -x.shape[-1] % LANES
    if short:
        x = jnp.concatenate([x, jnp.zeros((*x.shape[:-1], short), x.dtype)], -1)
    return x


def lon_block(tile, total, width, block):
    axis = 2
    count = -(-total // LANES)
    last = total % LANES
    start = block * width - 1
    c, off = start // LANES, start % LANES

    def piece(i):
        if i < 0:
            return pltpu.roll(tile(count - 1), (LANES - last) % LANES, axis)
        if i == count:
            return tile(0)
        x = tile(i)
        if i == count - 1 and last and total < start + width + 2:
            lane = lax.broadcasted_iota(jnp.int32, x.shape, axis)
            x = jnp.where(lane < last, x, pltpu.roll(tile(0), last, axis))
        return x

    x = piece(c)
    if off + width + 2 > LANES:
        lane = lax.broadcasted_iota(jnp.int32, x.shape, axis)
        x = jnp.where(lane >= off, x, piece(c + 1))
    return pltpu.roll(x, (2 * LANES - off - 1) % LANES, axis)


def spare(lane, width):
    return (lane > width) & (lane < LANES - 1)


def stow(x, d, width, p):
    free = LANES - 2 - width
    lane = lax.broadcasted_iota(jnp.int32, x.shape, 2)
    return jnp.where(spare(lane, width), pltpu.roll(d, (width + 2 - p * free) % LANES, 2), x)


def unstow(parts, width):
    free = LANES - 2 - width
    back = [pltpu.roll(x, (p * free - width - 2) % LANES, 2) for p, x in enumerate(parts)]
    lane = lax.broadcasted_iota(jnp.int32, back[0].shape, 2)
    later = jnp.where(lane < 2 * free - 1, back[1], back[2])
    return jnp.where((lane < free - 1) | (lane == LANES - 1), back[0], later)


def kernel(
    n_lat, n_lev,
    q_hbm, mc_hbm, temp_hbm, span_hbm, fall_hbm, zc_hbm, rate_hbm,
    out_ref, height_ref,
    q_ref, mc_ref, temp_ref, span_ref, fall_ref, zc_ref, rate_ref,
    main_s, main_r, thick_s, thick_r, north_s, north_r, south_s, south_r,
    tot_s, tot_r, zc_s, zc_r, inverse, kron, dens,
    main_ss, main_rs, thick_ss, thick_rs, north_ss, north_rs, south_ss, south_rs,
    tot_ss, tot_rs, zc_sem, own_sem, load_sem,
):
    i, j = lax.axis_index("lat"), lax.axis_index("lev")
    loads = [
        pltpu.make_async_copy(src, dst, load_sem.at[number])
        for number, (src, dst) in enumerate((
            (span_hbm, span_ref), (temp_hbm, temp_ref), (zc_hbm, zc_ref), (mc_hbm, mc_ref),
            (q_hbm, q_ref), (fall_hbm, fall_ref), (rate_hbm, rate_ref)))
    ]
    for load in loads:
        load.start()
    bins, rows, levels, total = q_ref.shape
    width = total // n_lev
    left, right = lax.rem(j + n_lev - 1, n_lev), lax.rem(j + 1, n_lev)
    has_south, has_north = i > 0, i < n_lat - 1

    barrier = pltpu.get_barrier_semaphore()
    for d in range(1, n_lev):
        pl.semaphore_signal(barrier, inc=1, device_id=(i, lax.rem(j + d, n_lev)), device_id_type=MESH)

    @pl.when(has_south)
    def _():
        for m in range(n_lev):
            pl.semaphore_signal(barrier, inc=1, device_id=(i - 1, m), device_id_type=MESH)

    @pl.when(has_north)
    def _():
        for m in range(n_lev):
            pl.semaphore_signal(barrier, inc=1, device_id=(i + 1, m), device_id_type=MESH)

    for load in loads[:3]:
        load.wait()
    thick = [specific_air_factor * temp_ref[:, k, :] * span_ref[k] for k in range(levels)]
    tot = thick[0]
    for k in range(1, levels):
        tot = tot + thick[k]
    tot_s[...] = widen(tot)
    for m in range(n_lev):
        for k in range(levels):
            wide = widen(thick[k])[None]
            tile = lambda c: wide[:, :, c * LANES : (c + 1) * LANES]
            thick_s[m, k] = lon_block(tile, total, width, m)[0]
    zc_s[...] = widen(zc_ref[...])

    peers = n_lev - 1 + n_lev * (jnp.minimum(i, 1) + jnp.minimum(n_lat - 1 - i, 1))
    pl.semaphore_wait(barrier, peers)

    def thick_copy(m):
        return pltpu.make_async_remote_copy(
            thick_s.at[m], thick_r.at[j], thick_ss.at[m], thick_rs.at[j], (i, m), MESH)

    def main_copy(m):
        return pltpu.make_async_remote_copy(
            main_s.at[m], main_r.at[j], main_ss.at[m], main_rs.at[j], (i, m), MESH)

    def tot_copy(m):
        return pltpu.make_async_remote_copy(
            tot_s, tot_r.at[j], tot_ss.at[m], tot_rs.at[j], (i, m), MESH)

    def north_copy(m):
        return pltpu.make_async_remote_copy(
            north_s.at[m], north_r.at[j], north_ss.at[m], north_rs.at[j], (i + 1, m), MESH)

    def south_copy(m):
        return pltpu.make_async_remote_copy(
            south_s.at[m], south_r.at[j], south_ss.at[m], south_rs.at[j], (i - 1, m), MESH)

    zc_copy = pltpu.make_async_remote_copy(
        zc_s, zc_r, zc_sem.at[0], zc_sem.at[1], (i, left), MESH)

    for m in range(n_lev):
        @pl.when(j != m)
        def _():
            thick_copy(m).start()
    zc_copy.start()

    def tile_of(ref, k):
        def tile(c):
            stop = min((c + 1) * LANES, total)
            return widen(ref[:, :, k, c * LANES : stop])
        return tile

    def mc_tile(k):
        def tile(c):
            stop = min((c + 1) * LANES, total)
            return widen(mc_ref[:, k, c * LANES : stop])[None]
        return tile

    for load in loads[3:5]:
        load.wait()
    group = bins // 4

    def send_block(m):
        for k in range(levels):
            x = lon_block(tile_of(q_ref, k), total, width, m)
            for p in range(3):
                main_s[m, k, pl.ds(p * group, group)] = stow(
                    x[p * group : (p + 1) * group], x[3 * group :], width, p)
            main_s[m, k, pl.ds(3 * group, 1)] = lon_block(mc_tile(k), total, width, m)

        @pl.when(j != m)
        def _():
            main_copy(m).start()

        for k in range(levels):
            south_s[m, k] = main_s[m, k, :, 0, :]
            north_s[m, k] = main_s[m, k, :, rows - 1, :]

        @pl.when(has_south)
        def _():
            south_copy(m).start()

        @pl.when(has_north)
        def _():
            north_copy(m).start()

    half_way = n_lev // 2

    @pl.when(j >= half_way)
    def _():
        for m in range(n_lev):
            send_block(m)

    @pl.when(j < half_way)
    def _():
        for m in range(n_lev):
            send_block((m + half_way) % n_lev)

    for m in range(n_lev):
        @pl.when(j > m)
        def _():
            tot_copy(m).start()

    own = [pltpu.make_async_copy(main_s.at[j], main_r.at[j], own_sem.at[0]),
           pltpu.make_async_copy(thick_s.at[j], thick_r.at[j], own_sem.at[1])]
    for copy in own:
        copy.start()

    @pl.when(jnp.logical_not(has_south))
    def _():
        north_r[...] = jnp.zeros_like(north_r)

    @pl.when(jnp.logical_not(has_north))
    def _():
        south_r[...] = jnp.zeros_like(south_r)

    for load in loads[5:]:
        load.wait()
    rate = rate_ref[...]
    r0 = lax.broadcasted_iota(jnp.int32, rate.shape, 0)
    r1 = lax.broadcasted_iota(jnp.int32, rate.shape, 1)
    merging = jnp.where(r1 < r0, rate, jnp.where(r1 > r0, -rate, 0.0))
    cells = bins * rows
    e0 = lax.broadcasted_iota(jnp.int32, (cells, bins), 0)
    e1 = lax.broadcasted_iota(jnp.int32, (cells, bins), 1)
    spread = jnp.where((e0 >= e1 * rows) & (e0 < (e1 + 1) * rows), 1.0, 0.0)
    half = jnp.dot(spread, merging, precision=HIGHEST, preferred_element_type=jnp.float32)
    full = lax.dot_general(half, spread, (((1,), (1,)), ((), ())), precision=HIGHEST,
                           preferred_element_type=jnp.float32)
    k0 = lax.broadcasted_iota(jnp.int32, full.shape, 0)
    k1 = lax.broadcasted_iota(jnp.int32, full.shape, 1)
    kron[...] = jnp.where(lax.rem(k0, rows) == lax.rem(k1, rows), full, 0.0)

    own[1].wait()
    for m in range(n_lev):
        @pl.when(j != m)
        def _():
            pltpu.make_async_remote_copy(
                thick_s.at[m], thick_r.at[m], thick_ss.at[m], thick_rs.at[m], (i, m), MESH).wait_recv()
    below = jnp.zeros((rows, LANES), jnp.float32)
    for k in reversed(range(n_lev * levels)):
        t = thick_r[k // levels, k % levels]
        dens[k] = jnp.exp((below + 0.5 * t) * (-1.0 / scale_height))
        below = below + t
        for b in range(bins):
            inverse[k, b] = 1.0 / (t + fall_ref[b])

    own[0].wait()
    zc_copy.wait_recv()

    flow = jnp.zeros((bins, rows, LANES), jnp.float32)
    sub = lax.broadcasted_iota(jnp.int32, (1, rows, LANES), 1)
    lane = lax.broadcasted_iota(jnp.int32, (1, rows, LANES), 2)
    for m in range(n_lev):
        @pl.when(j != m)
        def _():
            pltpu.make_async_remote_copy(
                main_s.at[m], main_r.at[m], main_ss.at[m], main_rs.at[m], (i, m), MESH).wait_recv()

        @pl.when(has_south)
        def _():
            pltpu.make_async_remote_copy(
                north_s.at[m], north_r.at[m], north_ss.at[m], north_rs.at[m], (i - 1, m), MESH).wait_recv()

        @pl.when(has_north)
        def _():
            pltpu.make_async_remote_copy(
                south_s.at[m], south_r.at[m], south_ss.at[m], south_rs.at[m], (i + 1, m), MESH).wait_recv()

        for kk in range(levels):
            k = m * levels + kk
            q = main_r[m, kk, pl.ds(0, 3 * group)].reshape(3, group, rows, LANES)
            mc = main_r[m, kk, pl.ds(3 * group, 1)]
            t = thick_r[m, pl.ds(kk, 1)]
            q_below = north_r[m, kk, pl.ds(0, 3 * group)].reshape(3, group, 1, LANES)
            q_above = south_r[m, kk, pl.ds(0, 3 * group)].reshape(3, group, 1, LANES)
            mc_above = south_r[m, kk, pl.ds(3 * group, 1)][:, None, :]
            mc_n = jnp.where(sub == rows - 1, mc_above, pltpu.roll(mc, rows - 1, 1))
            parts = []
            for p in range(3):
                c_s, c_n = stow(mc, mc, width, p), stow(mc_n, mc_n, width, p)
                x = q[p]
                q_s = jnp.where(sub == 0, q_below[p], pltpu.roll(x, 1, 1))
                q_n = jnp.where(sub == rows - 1, q_above[p], pltpu.roll(x, rows - 1, 1))
                south = jnp.maximum(c_s, 0.0) * q_s + jnp.minimum(c_s, 0.0) * x
                north = jnp.maximum(c_n, 0.0) * x + jnp.minimum(c_n, 0.0) * q_n
                parts.append(x + south - north)
            parts.append(unstow(parts, width))
            summed = jnp.concatenate(parts, 0) + flow
            settled = (t * inverse[k]) * summed
            flow = summed - settled
            z = jnp.where(lane == width, pltpu.roll(zc_r[:, k, :][None], width, 2), zc_s[:, k, :][None])
            west = jnp.maximum(z, 0.0) * pltpu.roll(settled, 1, 2) + jnp.minimum(z, 0.0) * settled
            moved = settled + west - pltpu.roll(west, LANES - 1, 2)
            coag = jnp.dot(kron[...], moved.reshape(cells, LANES), precision=HIGHEST,
                           preferred_element_type=jnp.float32).reshape(moved.shape)
            result = moved + dens[pl.ds(k, 1)] * moved * coag
            out_ref[:, :, k, :] = result[:, :, :width]

    below = jnp.zeros((rows, total), jnp.float32)
    for m in range(n_lev):
        @pl.when(j >= m)
        def _():
            tot_r[m] = jnp.zeros_like(tot_s)

        @pl.when(j < m)
        def _():
            pltpu.make_async_remote_copy(
                tot_s, tot_r.at[m], tot_ss.at[m], tot_rs.at[m], (i, m), MESH).wait_recv()

        below = below + tot_r[m][:, :total]
    for k in reversed(range(levels)):
        t = specific_air_factor * temp_ref[:, k, :] * span_ref[k]
        height_ref[:, k, :] = below + 0.5 * t
        below = below + t

    zc_copy.wait_send()
    for m in range(n_lev):
        @pl.when(j != m)
        def _():
            thick_copy(m).wait_send()
            main_copy(m).wait_send()

        @pl.when(j > m)
        def _():
            tot_copy(m).wait_send()

        @pl.when(has_south)
        def _():
            south_copy(m).wait_send()

        @pl.when(has_north)
        def _():
            north_copy(m).wait_send()


def solution(mesh):
    n_lat, n_lev = mesh.shape["lat"], mesh.shape["lev"]
    vmem = pl.BlockSpec(memory_space=pltpu.VMEM)
    hbm = pl.BlockSpec(memory_space=pltpu.HBM)

    def on_device(q, mc, temp, span, fall, zc, rate):
        bins, rows, levels, total = q.shape
        width = total // n_lev
        assert width + 2 <= 3 * (LANES - 2 - width) and bins % 4 == 0
        packed = 3 * bins // 4 + 1
        deep = n_lev * levels
        wide = -(-total // LANES) * LANES
        f32 = jnp.float32
        main = pltpu.VMEM((n_lev, levels, packed, rows, LANES), f32)
        thick = pltpu.VMEM((n_lev, levels, rows, LANES), f32)
        edge = pltpu.VMEM((n_lev, levels, packed, LANES), f32)
        zonal = pltpu.VMEM((rows, deep, LANES), f32)
        sems = pltpu.SemaphoreType.DMA((n_lev,))
        pair = pltpu.SemaphoreType.DMA((2,))
        return pl.pallas_call(
            functools.partial(kernel, n_lat, n_lev),
            out_shape=(
                jax.ShapeDtypeStruct((bins, rows, deep, width), f32),
                jax.ShapeDtypeStruct((rows, levels, total), f32),
            ),
            in_specs=[hbm] * 7,
            out_specs=(vmem, vmem),
            scratch_shapes=[
                pltpu.VMEM(q.shape, f32), pltpu.VMEM(mc.shape, f32), pltpu.VMEM(temp.shape, f32),
                pltpu.SMEM(span.shape, f32), pltpu.SMEM(fall.shape, f32),
                pltpu.VMEM(zc.shape, f32), pltpu.VMEM(rate.shape, f32),
                main, main, thick, thick, edge, edge, edge, edge,
                pltpu.VMEM((rows, wide), f32), pltpu.VMEM((n_lev, rows, wide), f32),
                zonal, zonal,
                pltpu.VMEM((deep, bins, rows, LANES), f32),
                pltpu.VMEM((bins * rows, bins * rows), f32),
                pltpu.VMEM((deep, rows, LANES), f32),
            ] + [sems] * 10 + [pair] * 2 + [pltpu.SemaphoreType.DMA((7,))],
            compiler_params=pltpu.CompilerParams(
                collective_id=0, has_side_effects=True, vmem_limit_bytes=63 * 1024 * 1024),
        )(q, mc, temp, span, fall, zc, rate)

    in_specs = (
        P(None, "lat", "lev", None),
        P("lat", "lev", None),
        P("lat", "lev", None),
        P("lev"),
        P(),
        P("lat", None, "lev"),
        P(),
    )
    out_specs = (P(None, "lat", None, "lev"), P("lat", "lev", None))
    return jax.shard_map(
        on_device, mesh=mesh, in_specs=in_specs, out_specs=out_specs, check_vma=False
    )
```

```python
import functools

import jax
import jax.numpy as jnp
from jax import lax
from jax.experimental import pallas as pl
from jax.experimental.pallas import tpu as pltpu
from jax.sharding import PartitionSpec as P

specific_air_factor = 0.0293
scale_height = 7.0
LANES = 128
MESH = pl.DeviceIdType.MESH
HIGHEST = lax.Precision.HIGHEST


def widen(x):
    short = -x.shape[-1] % LANES
    if short:
        x = jnp.concatenate([x, jnp.zeros((*x.shape[:-1], short), x.dtype)], -1)
    return x


def lon_block(tile, total, width, block):
    axis = 2
    count = -(-total // LANES)
    last = total % LANES
    start = block * width - 1
    c, off = start // LANES, start % LANES

    def piece(i):
        if i < 0:
            return pltpu.roll(tile(count - 1), (LANES - last) % LANES, axis)
        if i == count:
            return tile(0)
        x = tile(i)
        if i == count - 1 and last and total < start + width + 2:
            lane = lax.broadcasted_iota(jnp.int32, x.shape, axis)
            x = jnp.where(lane < last, x, pltpu.roll(tile(0), last, axis))
        return x

    x = piece(c)
    if off + width + 2 > LANES:
        lane = lax.broadcasted_iota(jnp.int32, x.shape, axis)
        x = jnp.where(lane >= off, x, piece(c + 1))
    return pltpu.roll(x, (2 * LANES - off - 1) % LANES, axis)


def spare(lane, width):
    return (lane > width) & (lane < LANES - 1)


def stow(x, d, width, p):
    free = LANES - 2 - width
    lane = lax.broadcasted_iota(jnp.int32, x.shape, 2)
    return jnp.where(spare(lane, width), pltpu.roll(d, (width + 2 - p * free) % LANES, 2), x)


def unstow(parts, width):
    free = LANES - 2 - width
    back = [pltpu.roll(x, (p * free - width - 2) % LANES, 2) for p, x in enumerate(parts)]
    lane = lax.broadcasted_iota(jnp.int32, back[0].shape, 2)
    later = jnp.where(lane < 2 * free - 1, back[1], back[2])
    return jnp.where((lane < free - 1) | (lane == LANES - 1), back[0], later)


def kernel(
    n_lat, n_lev,
    q_hbm, mc_hbm, temp_hbm, span_hbm, fall_hbm, zc_hbm, rate_hbm,
    out_ref, height_ref,
    q_ref, mc_ref, temp_ref, span_ref, fall_ref, zc_ref, rate_ref,
    main_s, main_r, thick_s, thick_r, north_s, north_r, south_s, south_r,
    tot_s, tot_r, zc_s, zc_r, inverse, advected, kron, dens,
    main_ss, main_rs, thick_ss, thick_rs, north_ss, north_rs, south_ss, south_rs,
    tot_ss, tot_rs, zc_sem, own_sem, load_sem,
):
    i, j = lax.axis_index("lat"), lax.axis_index("lev")
    loads = [
        pltpu.make_async_copy(src, dst, load_sem.at[number])
        for number, (src, dst) in enumerate((
            (span_hbm, span_ref), (temp_hbm, temp_ref), (zc_hbm, zc_ref), (mc_hbm, mc_ref),
            (q_hbm, q_ref), (fall_hbm, fall_ref), (rate_hbm, rate_ref)))
    ]
    for load in loads:
        load.start()
    bins, rows, levels, total = q_ref.shape
    width = total // n_lev
    left, right = lax.rem(j + n_lev - 1, n_lev), lax.rem(j + 1, n_lev)
    has_south, has_north = i > 0, i < n_lat - 1

    barrier = pltpu.get_barrier_semaphore()
    for d in range(1, n_lev):
        pl.semaphore_signal(barrier, inc=1, device_id=(i, lax.rem(j + d, n_lev)), device_id_type=MESH)

    @pl.when(has_south)
    def _():
        for m in range(n_lev):
            pl.semaphore_signal(barrier, inc=1, device_id=(i - 1, m), device_id_type=MESH)

    @pl.when(has_north)
    def _():
        for m in range(n_lev):
            pl.semaphore_signal(barrier, inc=1, device_id=(i + 1, m), device_id_type=MESH)

    for load in loads[:3]:
        load.wait()
    thick = [specific_air_factor * temp_ref[:, k, :] * span_ref[k] for k in range(levels)]
    tot = thick[0]
    for k in range(1, levels):
        tot = tot + thick[k]
    tot_s[...] = widen(tot)
    for m in range(n_lev):
        for k in range(levels):
            wide = widen(thick[k])[None]
            tile = lambda c: wide[:, :, c * LANES : (c + 1) * LANES]
            thick_s[m, k] = lon_block(tile, total, width, m)[0]
    zc_s[...] = widen(zc_ref[...])

    peers = n_lev - 1 + n_lev * (jnp.minimum(i, 1) + jnp.minimum(n_lat - 1 - i, 1))

    def thick_copy(m):
        return pltpu.make_async_remote_copy(
            thick_s.at[m], thick_r.at[j], thick_ss.at[m], thick_rs.at[j], (i, m), MESH)

    def main_copy(m):
        return pltpu.make_async_remote_copy(
            main_s.at[m], main_r.at[j], main_ss.at[m], main_rs.at[j], (i, m), MESH)

    def tot_copy(m):
        return pltpu.make_async_remote_copy(
            tot_s, tot_r.at[j], tot_ss.at[m], tot_rs.at[j], (i, m), MESH)

    def north_copy(m):
        return pltpu.make_async_remote_copy(
            north_s.at[m], north_r.at[j], north_ss.at[m], north_rs.at[j], (i + 1, m), MESH)

    def south_copy(m):
        return pltpu.make_async_remote_copy(
            south_s.at[m], south_r.at[j], south_ss.at[m], south_rs.at[j], (i - 1, m), MESH)

    zc_copy = pltpu.make_async_remote_copy(
        zc_s, zc_r, zc_sem.at[0], zc_sem.at[1], (i, left), MESH)

    def tile_of(ref, k):
        def tile(c):
            stop = min((c + 1) * LANES, total)
            return widen(ref[:, :, k, c * LANES : stop])
        return tile

    def mc_tile(k):
        def tile(c):
            stop = min((c + 1) * LANES, total)
            return widen(mc_ref[:, k, c * LANES : stop])[None]
        return tile

    for load in loads[3:5]:
        load.wait()
    group = bins // 4

    def cut_block(m):
        for k in range(levels):
            x = lon_block(tile_of(q_ref, k), total, width, m)
            for p in range(3):
                main_s[m, k, pl.ds(p * group, group)] = stow(
                    x[p * group : (p + 1) * group], x[3 * group :], width, p)
            main_s[m, k, pl.ds(3 * group, 1)] = lon_block(mc_tile(k), total, width, m)
            south_s[m, k] = main_s[m, k, :, 0, :]
            north_s[m, k] = main_s[m, k, :, rows - 1, :]

    def send_edges(m):
        @pl.when(has_south)
        def _():
            south_copy(m).start()

        @pl.when(has_north)
        def _():
            north_copy(m).start()

    half_way = n_lev // 2
    base = half_way * (j // half_way)

    def cut_half(first):
        for m in range(first, first + half_way):
            cut_block(m)

    @pl.when(j >= half_way)
    def _():
        cut_half(0)

    @pl.when(j < half_way)
    def _():
        cut_half(half_way)

    pl.semaphore_wait(barrier, peers)

    for m in range(n_lev):
        @pl.when(j != m)
        def _():
            thick_copy(m).start()
    for s in range(half_way):
        main_copy(half_way - base + s).start()
    for s in range(half_way):
        send_edges(half_way - base + s)
    zc_copy.start()

    @pl.when(j >= half_way)
    def _():
        cut_half(half_way)

    @pl.when(j < half_way)
    def _():
        cut_half(0)

    for s in range(half_way):
        m = base + s

        @pl.when(j != m)
        def _():
            main_copy(m).start()
        send_edges(m)

    for m in range(n_lev):
        @pl.when(j > m)
        def _():
            tot_copy(m).start()

    own = [pltpu.make_async_copy(main_s.at[j], main_r.at[j], own_sem.at[0]),
           pltpu.make_async_copy(thick_s.at[j], thick_r.at[j], own_sem.at[1])]
    for copy in own:
        copy.start()

    @pl.when(jnp.logical_not(has_south))
    def _():
        north_r[...] = jnp.zeros_like(north_r)

    @pl.when(jnp.logical_not(has_north))
    def _():
        south_r[...] = jnp.zeros_like(south_r)

    for load in loads[5:]:
        load.wait()
    rate = rate_ref[...]
    r0 = lax.broadcasted_iota(jnp.int32, rate.shape, 0)
    r1 = lax.broadcasted_iota(jnp.int32, rate.shape, 1)
    merging = jnp.where(r1 < r0, rate, jnp.where(r1 > r0, -rate, 0.0))
    cells = bins * rows
    e0 = lax.broadcasted_iota(jnp.int32, (cells, bins), 0)
    e1 = lax.broadcasted_iota(jnp.int32, (cells, bins), 1)
    spread = jnp.where((e0 >= e1 * rows) & (e0 < (e1 + 1) * rows), 1.0, 0.0)
    half = jnp.dot(spread, merging, precision=HIGHEST, preferred_element_type=jnp.float32)
    full = lax.dot_general(half, spread, (((1,), (1,)), ((), ())), precision=HIGHEST,
                           preferred_element_type=jnp.float32)
    k0 = lax.broadcasted_iota(jnp.int32, full.shape, 0)
    k1 = lax.broadcasted_iota(jnp.int32, full.shape, 1)
    kron[...] = jnp.where(lax.rem(k0, rows) == lax.rem(k1, rows), full, 0.0)

    own[1].wait()
    for m in range(n_lev):
        @pl.when(j != m)
        def _():
            pltpu.make_async_remote_copy(
                thick_s.at[m], thick_r.at[m], thick_ss.at[m], thick_rs.at[m], (i, m), MESH).wait_recv()
    below = jnp.zeros((rows, LANES), jnp.float32)
    for k in reversed(range(n_lev * levels)):
        t = thick_r[k // levels, k % levels]
        dens[k] = jnp.exp((below + 0.5 * t) * (-1.0 / scale_height))
        below = below + t
        for b in range(bins):
            inverse[k, b] = 1.0 / (t + fall_ref[b])

    own[0].wait()

    sub = lax.broadcasted_iota(jnp.int32, (1, rows, LANES), 1)
    lane = lax.broadcasted_iota(jnp.int32, (1, rows, LANES), 2)
    for s in range(n_lev):
        m = lax.rem(base + s, n_lev)

        @pl.when(j != m)
        def _():
            pltpu.make_async_remote_copy(
                main_s.at[m], main_r.at[m], main_ss.at[m], main_rs.at[m], (i, m), MESH).wait_recv()

        @pl.when(has_south)
        def _():
            pltpu.make_async_remote_copy(
                north_s.at[m], north_r.at[m], north_ss.at[m], north_rs.at[m], (i - 1, m), MESH).wait_recv()

        @pl.when(has_north)
        def _():
            pltpu.make_async_remote_copy(
                south_s.at[m], south_r.at[m], south_ss.at[m], south_rs.at[m], (i + 1, m), MESH).wait_recv()

        for kk in range(levels):
            q = main_r[m, kk, pl.ds(0, 3 * group)].reshape(3, group, rows, LANES)
            mc = main_r[m, kk, pl.ds(3 * group, 1)]
            q_below = north_r[m, kk, pl.ds(0, 3 * group)].reshape(3, group, 1, LANES)
            q_above = south_r[m, kk, pl.ds(0, 3 * group)].reshape(3, group, 1, LANES)
            mc_above = south_r[m, kk, pl.ds(3 * group, 1)][:, None, :]
            mc_n = jnp.where(sub == rows - 1, mc_above, pltpu.roll(mc, rows - 1, 1))
            parts = []
            for p in range(3):
                c_s, c_n = stow(mc, mc, width, p), stow(mc_n, mc_n, width, p)
                x = q[p]
                q_s = jnp.where(sub == 0, q_below[p], pltpu.roll(x, 1, 1))
                q_n = jnp.where(sub == rows - 1, q_above[p], pltpu.roll(x, rows - 1, 1))
                south = jnp.maximum(c_s, 0.0) * q_s + jnp.minimum(c_s, 0.0) * x
                north = jnp.maximum(c_n, 0.0) * x + jnp.minimum(c_n, 0.0) * q_n
                parts.append(x + south - north)
            parts.append(unstow(parts, width))
            for p in range(4):
                advected[m * levels + kk, pl.ds(p * group, group)] = parts[p]

    zc_copy.wait_recv()
    flow = jnp.zeros((bins, rows, LANES), jnp.float32)
    for k in range(n_lev * levels):
        t = thick_r[k // levels, pl.ds(k % levels, 1)]
        summed = advected[k] + flow
        settled = (t * inverse[k]) * summed
        flow = summed - settled
        z = jnp.where(lane == width, pltpu.roll(zc_r[:, k, :][None], width, 2), zc_s[:, k, :][None])
        west = jnp.maximum(z, 0.0) * pltpu.roll(settled, 1, 2) + jnp.minimum(z, 0.0) * settled
        moved = settled + west - pltpu.roll(west, LANES - 1, 2)
        coag = jnp.dot(kron[...], moved.reshape(cells, LANES), precision=HIGHEST,
                       preferred_element_type=jnp.float32).reshape(moved.shape)
        result = moved + dens[pl.ds(k, 1)] * moved * coag
        out_ref[:, :, k, :] = result[:, :, :width]

    below = jnp.zeros((rows, total), jnp.float32)
    for m in range(n_lev):
        @pl.when(j >= m)
        def _():
            tot_r[m] = jnp.zeros_like(tot_s)

        @pl.when(j < m)
        def _():
            pltpu.make_async_remote_copy(
                tot_s, tot_r.at[m], tot_ss.at[m], tot_rs.at[m], (i, m), MESH).wait_recv()

        below = below + tot_r[m][:, :total]
    for k in reversed(range(levels)):
        t = specific_air_factor * temp_ref[:, k, :] * span_ref[k]
        height_ref[:, k, :] = below + 0.5 * t
        below = below + t

    zc_copy.wait_send()
    for m in range(n_lev):
        @pl.when(j != m)
        def _():
            thick_copy(m).wait_send()
            main_copy(m).wait_send()

        @pl.when(j > m)
        def _():
            tot_copy(m).wait_send()

        @pl.when(has_south)
        def _():
            south_copy(m).wait_send()

        @pl.when(has_north)
        def _():
            north_copy(m).wait_send()


def solution(mesh):
    n_lat, n_lev = mesh.shape["lat"], mesh.shape["lev"]
    vmem = pl.BlockSpec(memory_space=pltpu.VMEM)
    hbm = pl.BlockSpec(memory_space=pltpu.HBM)

    def on_device(q, mc, temp, span, fall, zc, rate):
        bins, rows, levels, total = q.shape
        width = total // n_lev
        assert width + 2 <= 3 * (LANES - 2 - width) and bins % 4 == 0
        packed = 3 * bins // 4 + 1
        deep = n_lev * levels
        wide = -(-total // LANES) * LANES
        f32 = jnp.float32
        main = pltpu.VMEM((n_lev, levels, packed, rows, LANES), f32)
        thick = pltpu.VMEM((n_lev, levels, rows, LANES), f32)
        edge = pltpu.VMEM((n_lev, levels, packed, LANES), f32)
        zonal = pltpu.VMEM((rows, deep, LANES), f32)
        sems = pltpu.SemaphoreType.DMA((n_lev,))
        pair = pltpu.SemaphoreType.DMA((2,))
        return pl.pallas_call(
            functools.partial(kernel, n_lat, n_lev),
            out_shape=(
                jax.ShapeDtypeStruct((bins, rows, deep, width), f32),
                jax.ShapeDtypeStruct((rows, levels, total), f32),
            ),
            in_specs=[hbm] * 7,
            out_specs=(vmem, vmem),
            scratch_shapes=[
                pltpu.VMEM(q.shape, f32), pltpu.VMEM(mc.shape, f32), pltpu.VMEM(temp.shape, f32),
                pltpu.SMEM(span.shape, f32), pltpu.SMEM(fall.shape, f32),
                pltpu.VMEM(zc.shape, f32), pltpu.VMEM(rate.shape, f32),
                main, main, thick, thick, edge, edge, edge, edge,
                pltpu.VMEM((rows, wide), f32), pltpu.VMEM((n_lev, rows, wide), f32),
                zonal, zonal,
                pltpu.VMEM((deep, bins, rows, LANES), f32),
                pltpu.VMEM((deep, bins, rows, LANES), f32),
                pltpu.VMEM((bins * rows, bins * rows), f32),
                pltpu.VMEM((deep, rows, LANES), f32),
            ] + [sems] * 10 + [pair] * 2 + [pltpu.SemaphoreType.DMA((7,))],
            compiler_params=pltpu.CompilerParams(
                collective_id=0, has_side_effects=True, vmem_limit_bytes=63 * 1024 * 1024),
        )(q, mc, temp, span, fall, zc, rate)

    in_specs = (
        P(None, "lat", "lev", None),
        P("lat", "lev", None),
        P("lat", "lev", None),
        P("lev"),
        P(),
        P("lat", None, "lev"),
        P(),
    )
    out_specs = (P(None, "lat", None, "lev"), P("lat", "lev", None))
    return jax.shard_map(
        on_device, mesh=mesh, in_specs=in_specs, out_specs=out_specs, check_vma=False
    )
```

```python
import functools

import jax
import jax.numpy as jnp
from jax import lax
from jax.experimental import pallas as pl
from jax.experimental.pallas import tpu as pltpu
from jax.sharding import PartitionSpec as P

specific_air_factor = 0.0293
scale_height = 7.0
LANES = 128
MESH = pl.DeviceIdType.MESH
HIGHEST = lax.Precision.HIGHEST


def widen(x):
    short = -x.shape[-1] % LANES
    if short:
        x = jnp.concatenate([x, jnp.zeros((*x.shape[:-1], short), x.dtype)], -1)
    return x


def lon_block(tile, total, width, block):
    axis = 2
    count = -(-total // LANES)
    last = total % LANES
    start = block * width - 1
    c, off = start // LANES, start % LANES

    def piece(i):
        if i < 0:
            return pltpu.roll(tile(count - 1), (LANES - last) % LANES, axis)
        if i == count:
            return tile(0)
        x = tile(i)
        if i == count - 1 and last and total < start + width + 2:
            lane = lax.broadcasted_iota(jnp.int32, x.shape, axis)
            x = jnp.where(lane < last, x, pltpu.roll(tile(0), last, axis))
        return x

    x = piece(c)
    if off + width + 2 > LANES:
        lane = lax.broadcasted_iota(jnp.int32, x.shape, axis)
        x = jnp.where(lane >= off, x, piece(c + 1))
    return pltpu.roll(x, (2 * LANES - off - 1) % LANES, axis)


def spare(lane, width):
    return (lane > width) & (lane < LANES - 1)


def stow(x, d, width, p):
    free = LANES - 2 - width
    lane = lax.broadcasted_iota(jnp.int32, x.shape, 2)
    return jnp.where(spare(lane, width), pltpu.roll(d, (width + 2 - p * free) % LANES, 2), x)


def unstow(parts, width):
    free = LANES - 2 - width
    back = [pltpu.roll(x, (p * free - width - 2) % LANES, 2) for p, x in enumerate(parts)]
    lane = lax.broadcasted_iota(jnp.int32, back[0].shape, 2)
    later = jnp.where(lane < 2 * free - 1, back[1], back[2])
    return jnp.where((lane < free - 1) | (lane == LANES - 1), back[0], later)


def kernel(
    n_lat, n_lev,
    q_hbm, mc_hbm, temp_hbm, span_hbm, fall_hbm, zc_hbm, rate_hbm,
    out_ref, height_ref,
    q_ref, mc_ref, temp_ref, span_ref, fall_ref, zc_ref, rate_ref,
    main_s, main_r, thick_s, thick_r, north_s, north_r, south_s, south_r,
    tot_s, tot_r, zc_s, zc_r, inverse, advected, kron, dens,
    main_ss, main_rs, thick_ss, thick_rs, north_ss, north_rs, south_ss, south_rs,
    tot_ss, tot_rs, zc_sem, own_sem, load_sem,
):
    i, j = lax.axis_index("lat"), lax.axis_index("lev")
    loads = [
        pltpu.make_async_copy(src, dst, load_sem.at[number])
        for number, (src, dst) in enumerate((
            (span_hbm, span_ref), (temp_hbm, temp_ref), (zc_hbm, zc_ref), (mc_hbm, mc_ref),
            (q_hbm, q_ref), (fall_hbm, fall_ref), (rate_hbm, rate_ref)))
    ]
    for load in loads:
        load.start()
    bins, rows, levels, total = q_ref.shape
    width = total // n_lev
    left, right = lax.rem(j + n_lev - 1, n_lev), lax.rem(j + 1, n_lev)
    has_south, has_north = i > 0, i < n_lat - 1

    barrier = pltpu.get_barrier_semaphore()
    for d in range(1, n_lev):
        pl.semaphore_signal(barrier, inc=1, device_id=(i, lax.rem(j + d, n_lev)), device_id_type=MESH)

    @pl.when(has_south)
    def _():
        for m in range(n_lev):
            pl.semaphore_signal(barrier, inc=1, device_id=(i - 1, m), device_id_type=MESH)

    @pl.when(has_north)
    def _():
        for m in range(n_lev):
            pl.semaphore_signal(barrier, inc=1, device_id=(i + 1, m), device_id_type=MESH)

    for load in loads[:3]:
        load.wait()
    thick = [specific_air_factor * temp_ref[:, k, :] * span_ref[k] for k in range(levels)]
    tot = thick[0]
    for k in range(1, levels):
        tot = tot + thick[k]
    tot_s[...] = widen(tot)
    for m in range(n_lev):
        for k in range(levels):
            wide = widen(thick[k])[None]
            tile = lambda c: wide[:, :, c * LANES : (c + 1) * LANES]
            thick_s[m, k] = lon_block(tile, total, width, m)[0]
    zc_s[...] = widen(zc_ref[...])

    peers = n_lev - 1 + n_lev * (jnp.minimum(i, 1) + jnp.minimum(n_lat - 1 - i, 1))

    def thick_copy(m):
        return pltpu.make_async_remote_copy(
            thick_s.at[m], thick_r.at[j], thick_ss.at[m], thick_rs.at[j], (i, m), MESH)

    def main_copy(m):
        return pltpu.make_async_remote_copy(
            main_s.at[m], main_r.at[j], main_ss.at[m], main_rs.at[j], (i, m), MESH)

    def tot_copy(m):
        return pltpu.make_async_remote_copy(
            tot_s, tot_r.at[j], tot_ss.at[m], tot_rs.at[j], (i, m), MESH)

    def north_copy(m):
        return pltpu.make_async_remote_copy(
            north_s.at[m], north_r.at[j], north_ss.at[m], north_rs.at[j], (i + 1, m), MESH)

    def south_copy(m):
        return pltpu.make_async_remote_copy(
            south_s.at[m], south_r.at[j], south_ss.at[m], south_rs.at[j], (i - 1, m), MESH)

    zc_copy = pltpu.make_async_remote_copy(
        zc_s, zc_r, zc_sem.at[0], zc_sem.at[1], (i, left), MESH)

    def tile_of(ref, k):
        def tile(c):
            stop = min((c + 1) * LANES, total)
            return widen(ref[:, :, k, c * LANES : stop])
        return tile

    def mc_tile(k):
        def tile(c):
            stop = min((c + 1) * LANES, total)
            return widen(mc_ref[:, k, c * LANES : stop])[None]
        return tile

    for load in loads[3:5]:
        load.wait()
    group = bins // 4

    def cut_block(m):
        for k in range(levels):
            x = lon_block(tile_of(q_ref, k), total, width, m)
            for p in range(3):
                main_s[m, k, pl.ds(p * group, group)] = stow(
                    x[p * group : (p + 1) * group], x[3 * group :], width, p)
            main_s[m, k, pl.ds(3 * group, 1)] = lon_block(mc_tile(k), total, width, m)
            south_s[m, k] = main_s[m, k, :, 0, :]
            north_s[m, k] = main_s[m, k, :, rows - 1, :]

    def send_edges(m):
        @pl.when(has_south)
        def _():
            south_copy(m).start()

        @pl.when(has_north)
        def _():
            north_copy(m).start()

    half_way = n_lev // 2
    base = half_way * (j // half_way)

    def cut_half(first):
        for m in range(first, first + half_way):
            cut_block(m)

    @pl.when(j >= half_way)
    def _():
        cut_half(0)

    @pl.when(j < half_way)
    def _():
        cut_half(half_way)

    pl.semaphore_wait(barrier, peers)

    for m in range(n_lev):
        @pl.when(j != m)
        def _():
            thick_copy(m).start()
    for s in range(half_way):
        main_copy(half_way - base + s).start()
    for s in range(half_way):
        send_edges(half_way - base + s)
    zc_copy.start()

    @pl.when(j >= half_way)
    def _():
        cut_half(half_way)

    @pl.when(j < half_way)
    def _():
        cut_half(0)

    for s in range(half_way):
        m = base + s

        @pl.when(j != m)
        def _():
            main_copy(m).start()
        send_edges(m)

    for m in range(n_lev):
        @pl.when(j > m)
        def _():
            tot_copy(m).start()

    own = [pltpu.make_async_copy(main_s.at[j], main_r.at[j], own_sem.at[0]),
           pltpu.make_async_copy(thick_s.at[j], thick_r.at[j], own_sem.at[1])]
    for copy in own:
        copy.start()

    @pl.when(jnp.logical_not(has_south))
    def _():
        north_r[...] = jnp.zeros_like(north_r)

    @pl.when(jnp.logical_not(has_north))
    def _():
        south_r[...] = jnp.zeros_like(south_r)

    for load in loads[5:]:
        load.wait()
    rate = rate_ref[...]
    r0 = lax.broadcasted_iota(jnp.int32, rate.shape, 0)
    r1 = lax.broadcasted_iota(jnp.int32, rate.shape, 1)
    merging = jnp.where(r1 < r0, rate, jnp.where(r1 > r0, -rate, 0.0))
    cells = bins * rows
    e0 = lax.broadcasted_iota(jnp.int32, (cells, bins), 0)
    e1 = lax.broadcasted_iota(jnp.int32, (cells, bins), 1)
    spread = jnp.where((e0 >= e1 * rows) & (e0 < (e1 + 1) * rows), 1.0, 0.0)
    half = jnp.dot(spread, merging, precision=HIGHEST, preferred_element_type=jnp.float32)
    full = lax.dot_general(half, spread, (((1,), (1,)), ((), ())), precision=HIGHEST,
                           preferred_element_type=jnp.float32)
    k0 = lax.broadcasted_iota(jnp.int32, full.shape, 0)
    k1 = lax.broadcasted_iota(jnp.int32, full.shape, 1)
    kron[...] = jnp.where(lax.rem(k0, rows) == lax.rem(k1, rows), full, 0.0)

    own[1].wait()
    for m in range(n_lev):
        @pl.when(j != m)
        def _():
            pltpu.make_async_remote_copy(
                thick_s.at[m], thick_r.at[m], thick_ss.at[m], thick_rs.at[m], (i, m), MESH).wait_recv()
    below = jnp.zeros((rows, LANES), jnp.float32)
    for k in reversed(range(n_lev * levels)):
        t = thick_r[k // levels, k % levels]
        dens[k] = jnp.exp((below + 0.5 * t) * (-1.0 / scale_height))
        below = below + t
        for b in range(bins):
            inverse[k, b] = 1.0 / (t + fall_ref[b])

    own[0].wait()

    sub = lax.broadcasted_iota(jnp.int32, (1, rows, LANES), 1)
    lane = lax.broadcasted_iota(jnp.int32, (1, rows, LANES), 2)
    for s in range(n_lev):
        m = lax.rem(base + s, n_lev)

        @pl.when(j != m)
        def _():
            pltpu.make_async_remote_copy(
                main_s.at[m], main_r.at[m], main_ss.at[m], main_rs.at[m], (i, m), MESH).wait_recv()

        @pl.when(has_south)
        def _():
            pltpu.make_async_remote_copy(
                north_s.at[m], north_r.at[m], north_ss.at[m], north_rs.at[m], (i - 1, m), MESH).wait_recv()

        @pl.when(has_north)
        def _():
            pltpu.make_async_remote_copy(
                south_s.at[m], south_r.at[m], south_ss.at[m], south_rs.at[m], (i + 1, m), MESH).wait_recv()

        for kk in range(levels):
            q = main_r[m, kk, pl.ds(0, 3 * group)].reshape(3, group, rows, LANES)
            mc = main_r[m, kk, pl.ds(3 * group, 1)]
            q_below = north_r[m, kk, pl.ds(0, 3 * group)].reshape(3, group, 1, LANES)
            q_above = south_r[m, kk, pl.ds(0, 3 * group)].reshape(3, group, 1, LANES)
            mc_above = south_r[m, kk, pl.ds(3 * group, 1)][:, None, :]
            mc_n = jnp.where(sub == rows - 1, mc_above, pltpu.roll(mc, rows - 1, 1))
            parts = []
            for p in range(3):
                c_s, c_n = stow(mc, mc, width, p), stow(mc_n, mc_n, width, p)
                x = q[p]
                q_s = jnp.where(sub == 0, q_below[p], pltpu.roll(x, 1, 1))
                q_n = jnp.where(sub == rows - 1, q_above[p], pltpu.roll(x, rows - 1, 1))
                south = jnp.maximum(c_s, 0.0) * q_s + jnp.minimum(c_s, 0.0) * x
                north = jnp.maximum(c_n, 0.0) * x + jnp.minimum(c_n, 0.0) * q_n
                parts.append(x + south - north)
            parts.append(unstow(parts, width))
            for p in range(4):
                advected[m * levels + kk, pl.ds(p * group, group)] = parts[p]

    zc_copy.wait_recv()
    flow = jnp.zeros((bins, rows, LANES), jnp.float32)
    for k in range(n_lev * levels):
        t = thick_r[k // levels, pl.ds(k % levels, 1)]
        summed = advected[k] + flow
        settled = (t * inverse[k]) * summed
        flow = summed - settled
        z = jnp.where(lane == width, pltpu.roll(zc_r[:, k, :][None], width, 2), zc_s[:, k, :][None])
        west = jnp.maximum(z, 0.0) * pltpu.roll(settled, 1, 2) + jnp.minimum(z, 0.0) * settled
        moved = settled + west - pltpu.roll(west, LANES - 1, 2)
        coag = jnp.dot(kron[...], moved.reshape(cells, LANES), precision=HIGHEST,
                       preferred_element_type=jnp.float32).reshape(moved.shape)
        result = moved + dens[pl.ds(k, 1)] * moved * coag
        out_ref[:, :, k, :] = result[:, :, :width]

    below = jnp.zeros((rows, total), jnp.float32)
    for m in range(n_lev):
        @pl.when(j >= m)
        def _():
            tot_r[m] = jnp.zeros_like(tot_s)

        @pl.when(j < m)
        def _():
            pltpu.make_async_remote_copy(
                tot_s, tot_r.at[m], tot_ss.at[m], tot_rs.at[m], (i, m), MESH).wait_recv()

        below = below + tot_r[m][:, :total]
    for k in reversed(range(levels)):
        t = specific_air_factor * temp_ref[:, k, :] * span_ref[k]
        height_ref[:, k, :] = below + 0.5 * t
        below = below + t

    zc_copy.wait_send()
    for m in range(n_lev):
        @pl.when(j != m)
        def _():
            thick_copy(m).wait_send()
            main_copy(m).wait_send()

        @pl.when(j > m)
        def _():
            tot_copy(m).wait_send()

        @pl.when(has_south)
        def _():
            south_copy(m).wait_send()

        @pl.when(has_north)
        def _():
            north_copy(m).wait_send()


def hand_over(dust_ref, height_ref, dust_out, height_out, dust_v, height_v, sem_in, sem_out):
    pieces = sem_in.shape[0] - 1
    step = dust_ref.shape[0] // pieces
    arrive, leave = [], []
    for p in range(pieces):
        part = pl.ds(p * step, step)
        arrive.append(pltpu.make_async_copy(dust_ref.at[part], dust_v.at[part], sem_in.at[p]))
        leave.append(pltpu.make_async_copy(dust_v.at[part], dust_out.at[part], sem_out.at[p]))
    arrive.append(pltpu.make_async_copy(height_ref, height_v, sem_in.at[pieces]))
    leave.append(pltpu.make_async_copy(height_v, height_out, sem_out.at[pieces]))
    for copy in arrive:
        copy.start()
    for first, second in zip(arrive, leave):
        first.wait()
        second.start()
    for copy in leave:
        copy.wait()


def solution(mesh):
    n_lat, n_lev = mesh.shape["lat"], mesh.shape["lev"]
    vmem = pl.BlockSpec(memory_space=pltpu.VMEM)
    hbm = pl.BlockSpec(memory_space=pltpu.HBM)

    def on_device(q, mc, temp, span, fall, zc, rate):
        bins, rows, levels, total = q.shape
        width = total // n_lev
        assert width + 2 <= 3 * (LANES - 2 - width) and bins % 4 == 0
        packed = 3 * bins // 4 + 1
        deep = n_lev * levels
        wide = -(-total // LANES) * LANES
        f32 = jnp.float32
        main = pltpu.VMEM((n_lev, levels, packed, rows, LANES), f32)
        thick = pltpu.VMEM((n_lev, levels, rows, LANES), f32)
        edge = pltpu.VMEM((n_lev, levels, packed, LANES), f32)
        zonal = pltpu.VMEM((rows, deep, LANES), f32)
        sems = pltpu.SemaphoreType.DMA((n_lev,))
        pair = pltpu.SemaphoreType.DMA((2,))
        dust, height = pl.pallas_call(
            functools.partial(kernel, n_lat, n_lev),
            out_shape=(
                jax.ShapeDtypeStruct((bins, rows, deep, width), f32),
                jax.ShapeDtypeStruct((rows, levels, total), f32),
            ),
            in_specs=[hbm] * 7,
            out_specs=(vmem, vmem),
            scratch_shapes=[
                pltpu.VMEM(q.shape, f32), pltpu.VMEM(mc.shape, f32), pltpu.VMEM(temp.shape, f32),
                pltpu.SMEM(span.shape, f32), pltpu.SMEM(fall.shape, f32),
                pltpu.VMEM(zc.shape, f32), pltpu.VMEM(rate.shape, f32),
                main, main, thick, thick, edge, edge, edge, edge,
                pltpu.VMEM((rows, wide), f32), pltpu.VMEM((n_lev, rows, wide), f32),
                zonal, zonal,
                pltpu.VMEM((deep, bins, rows, LANES), f32),
                pltpu.VMEM((deep, bins, rows, LANES), f32),
                pltpu.VMEM((bins * rows, bins * rows), f32),
                pltpu.VMEM((deep, rows, LANES), f32),
            ] + [sems] * 10 + [pair] * 2 + [pltpu.SemaphoreType.DMA((7,))],
            compiler_params=pltpu.CompilerParams(
                collective_id=0, has_side_effects=True, vmem_limit_bytes=63 * 1024 * 1024),
        )(q, mc, temp, span, fall, zc, rate)
        return pl.pallas_call(
            hand_over,
            out_shape=(
                jax.ShapeDtypeStruct(dust.shape, f32), jax.ShapeDtypeStruct(height.shape, f32)),
            in_specs=[hbm, hbm],
            out_specs=(hbm, hbm),
            scratch_shapes=[
                pltpu.VMEM(dust.shape, f32), pltpu.VMEM(height.shape, f32),
                pltpu.SemaphoreType.DMA((5,)), pltpu.SemaphoreType.DMA((5,))],
            compiler_params=pltpu.CompilerParams(vmem_limit_bytes=63 * 1024 * 1024),
        )(dust, height)

    in_specs = (
        P(None, "lat", "lev", None),
        P("lat", "lev", None),
        P("lat", "lev", None),
        P("lev"),
        P(),
        P("lat", None, "lev"),
        P(),
    )
    out_specs = (P(None, "lat", None, "lev"), P("lat", "lev", None))
    return jax.shard_map(
        on_device, mesh=mesh, in_specs=in_specs, out_specs=out_specs, check_vma=False
    )
```
